32 devices in a mesh: dp: 8 (over z, y), tensor: 4 (over x, core).
Axes of the slice: x: 2, y: 2, z: 4, core: 2. Of those that a mesh axis runs over, the one named last changes fastest.
Arguments:
- tokens: bfloat16 [4096, 4096], P('dp', 'tensor'), may hold values from -6 to 6
- grad_out: bfloat16 [4096, 4096], P('dp'), may hold values from -3 to 3
- gate_pre: bfloat16 [4096, 14336], P('dp', 'tensor'), may hold values from -9 to 9
- up_value: bfloat16 [4096, 14336], P('dp', 'tensor'), may hold values from -6 to 6
- down_weight: bfloat16 [14336, 4096], P('tensor', 'dp'), may hold values from -0.09375 to 0.09375
- in_proj: bfloat16 [128, 4096], P(None, 'tensor'), may hold values from -0.09375 to 0.09375
- out_proj: bfloat16 [128, 14336], P(None, 'tensor'), may hold values from -0.046875 to 0.046875
- test_matrix: bfloat16 [16384, 128], replicated, may hold values from -0.046875 to 0.046875
Outputs:
- factor: float32 [16384, 128], P(('dp', 'tensor'))
The draws below stay inside these ranges and needn't reach their ends.
All inputs are finite; a program needn't handle non-finite values.
Results may differ from the reference program's by a relative error of at most 0.0065.
The reference program's roundings to bfloat16 on the way (of `gate_grad`, `act_low`, `out_low`, `proj_grad` and `coeff`) count: a program that leaves them out, or rounds other values in their place, can miss the bound.
Values may be sent and summed in bfloat16 or wider, within the bound.
No kernel may reach another device: no remote copies, remote signals or barrier semaphores. Data moves between devices by JAX's collectives and lax.ppermute only.
A program may use at most 128 MiB of HBM per device.

```python
import jax
import jax.numpy as jnp
from jax import lax

D = 4096
FF = 14336
PDIM = 128
RANK = 128
SEQ_LEN = 128
TOKENS = 4096
SEQS = 32
PROJ = 16384


def levels(rng, shape, cuts, low, high):
    gain = 1.0
    for dim, shards_of in cuts:
        heights = jax.random.uniform(jax.random.fold_in(jax.random.fold_in(rng, 6), dim), (shards_of,), jnp.float32, low / len(cuts), high / len(cuts))
        gain = gain * jnp.repeat(jnp.exp(heights), shape[dim] // shards_of).reshape((-1,) + (1,) * (len(shape) - 1 - dim))
    return gain


def noise(key, shape, deviation, bound, split=(), dtype=jnp.bfloat16):
    values = jax.random.normal(key, shape, jnp.float32) * deviation
    if len(split) > 0:
        values = levels(key, shape, split, -0.22, 0.18) * values
    return jnp.clip(values, min=-bound, max=bound).astype(dtype)


def setup_inputs(seed: int = 0) -> dict:
    key_of = jax.random.split(jax.random.key(seed), 9)
    tokens = noise(key_of[0], (TOKENS, D), 1.0, 6.0, ((0, 8), (1, 4)))
    grad_out = noise(key_of[1], (TOKENS, D), 0.5, 3.0, ((0, 8),))
    gate_pre = noise(key_of[2], (TOKENS, FF), 1.5, 9.0, ((0, 8), (1, 4)))
    up_value = noise(key_of[3], (TOKENS, FF), 1.0, 6.0, ((0, 8), (1, 4)))
    down_weight = noise(key_of[4], (FF, D), D ** -0.5, 0.09375, ((0, 4), (1, 8)))
    in_proj = noise(key_of[5], (PDIM, D), D ** -0.5, 0.09375, ((1, 4),))
    out_proj = noise(key_of[6], (PDIM, FF), FF ** -0.5, 0.046875, ((1, 4),))
    test_matrix = noise(key_of[7], (PROJ, RANK), PROJ ** -0.5, 0.046875)
    return {"tokens": tokens, "grad_out": grad_out, "gate_pre": gate_pre, "up_value": up_value, "down_weight": down_weight, "in_proj": in_proj, "out_proj": out_proj, "test_matrix": test_matrix}


def reference(tokens, grad_out, gate_pre, up_value, down_weight, in_proj, out_proj, test_matrix):
    hidden_grad = jnp.dot(grad_out.astype(jnp.float32), down_weight.T.astype(jnp.float32), preferred_element_type=jnp.float32)
    gate_wide = gate_pre.astype(jnp.float32)
    logistic = jax.nn.sigmoid(gate_wide)
    gate_grad = (hidden_grad * up_value.astype(jnp.float32) * logistic * (1.0 + gate_wide * (1.0 - logistic))).astype(jnp.bfloat16)
    act_low = jnp.dot(tokens.astype(jnp.float32), in_proj.T.astype(jnp.float32), preferred_element_type=jnp.float32).astype(jnp.bfloat16)
    out_low = jnp.dot(gate_grad.astype(jnp.float32), out_proj.T.astype(jnp.float32), preferred_element_type=jnp.float32).astype(jnp.bfloat16)
    act_seq = act_low.reshape(SEQS, SEQ_LEN, PDIM).astype(jnp.float32)
    out_seq = out_low.reshape(SEQS, SEQ_LEN, PDIM).astype(jnp.float32)
    proj_grad = jnp.einsum('slp,slq->spq', act_seq, out_seq).reshape(SEQS, PROJ).astype(jnp.bfloat16)
    coeff = jnp.dot(proj_grad.astype(jnp.float32), test_matrix.astype(jnp.float32), preferred_element_type=jnp.float32).astype(jnp.bfloat16)
    sketch = jnp.dot(proj_grad.T.astype(jnp.float32), coeff.astype(jnp.float32), preferred_element_type=jnp.float32)
    omega_wide = test_matrix.astype(jnp.float32)
    square_sum = jnp.sum(sketch * sketch)
    omega_sq = jnp.sum(omega_wide * omega_wide)
    shift = 0.1 * jnp.sqrt(square_sum / (omega_sq + 1e-06))
    shifted = sketch + shift * omega_wide
    core = jnp.dot(omega_wide.T, shifted, precision=lax.Precision.HIGHEST)
    core = 0.5 * (core + core.T)
    lower = jnp.linalg.cholesky(core)
    factor = jax.scipy.linalg.solve_triangular(lower, shifted.T, lower=True).T
    return factor
```

```python
import math

import jax
import jax.numpy as jnp
from jax import lax
from jax.sharding import Mesh, PartitionSpec as P

SEQ_LEN = 128
LINE = 4


shift_scale = 0.1
tiny_value = 1e-06

f32 = jnp.float32
bf16 = jnp.bfloat16


def swap(value, axis):
    if isinstance(axis, str):
        return lax.ppermute(value, axis, [(0, 1), (1, 0)])
    count = 2 ** len(axis)
    return lax.ppermute(value, axis, [(i, count - 1 - i) for i in range(count)])


def pick(value, index, dim):
    half = value.shape[dim] // 2
    return lax.dynamic_slice_in_dim(value, index * half, half, dim)


def dot_t(left, right):
    return lax.dot_general(left, right, (((1,), (1,)), ((), ())), preferred_element_type=f32)


def scatter_sum(part, x_index, c_index):
    kept = lax.dynamic_index_in_dim(part, c_index, 1, False)
    given = lax.dynamic_index_in_dim(part, 1 - c_index, 1, False)
    kept = kept + swap(given, "c")
    own = lax.dynamic_index_in_dim(kept, x_index, 0, False)
    other = lax.dynamic_index_in_dim(kept, 1 - x_index, 0, False)
    return own, other


def local(tokens, grad_out, gate_pre, up_value, down_weight, in_proj, out_proj, test_matrix):
    depth = lax.axis_size("z")
    z, y, x, c = (lax.axis_index(a) for a in ("z", "y", "x", "c"))
    rows = grad_out.shape[0]
    pdim = in_proj.shape[0]
    rank_cols = test_matrix.shape[1]
    seqs_here = rows // SEQ_LEN
    middle = lax.axis_size("m")
    chunk = down_weight.shape[1] * middle
    if middle > 1:
        down_weight = lax.all_gather(down_weight, "m", axis=1, tiled=True)
        grad_out = grad_out.reshape(rows, depth, middle, 2, -1).swapaxes(2, 3).reshape(rows, -1)

    keep_weight = pick(down_weight, y, 0)
    take_weight = swap(pick(down_weight, 1 - y, 0), "y")
    quarter = grad_out.shape[1] // 4
    sent = lax.dynamic_slice_in_dim(grad_out, (x * 2 + c) * quarter, quarter, 1)
    sent = swap(sent, "y")
    sent_x = swap(sent, "x")
    sent_c, sent_xc = swap(sent, "c"), swap(sent_x, "c")
    quarters = jnp.zeros_like(grad_out)
    for value, at in ((sent, x * 2 + c), (sent_x, (1 - x) * 2 + c), (sent_c, x * 2 + 1 - c), (sent_xc, (1 - x) * 2 + 1 - c)):
        quarters = lax.dynamic_update_slice_in_dim(quarters, value, at * quarter, 1)
    grad_both = jnp.concatenate((grad_out, quarters), 0)

    def both(value):
        return jnp.concatenate((pick(value, y, 1), swap(pick(value, 1 - y, 1), "y")), 0)

    gate_wide = both(gate_pre).astype(f32)
    up_wide = both(up_value).astype(f32)
    logistic = jax.nn.sigmoid(gate_wide)
    scale = up_wide * logistic * (1.0 + gate_wide * (1.0 - logistic))

    def term(piece, source, side):
        at = jnp.clip(source, 0, depth - 1) * 2 + side
        return dot_t(lax.dynamic_slice_in_dim(grad_both, at * chunk, chunk, 1), piece)

    up_moves = [(i, i + 1) for i in range(depth - 1)]
    down_moves = [(i + 1, i) for i in range(depth - 1)]
    hidden = term(keep_weight, z, y) + term(take_weight, z, 1 - y)
    rising = [keep_weight, take_weight]
    falling = [keep_weight, take_weight]
    for step in range(1, depth):
        for n, side in ((0, y), (1, 1 - y)):
            rising[n] = lax.ppermute(rising[n], "z", up_moves)
            falling[n] = lax.ppermute(falling[n], "z", down_moves)
            if 2 * step < depth:
                hidden = hidden + term(rising[n], z - step, side) + term(falling[n], z + step, side)
            else:
                from_low = z >= step
                hidden = hidden + term(
                    jnp.where(from_low, rising[n], falling[n]), jnp.where(from_low, z - step, z + step), side
                )
    gate_grad = (hidden * scale).astype(bf16)
    out_part = dot_t(gate_grad, pick(out_proj, y, 1))

    act_part = dot_t(tokens, in_proj)
    act_own, act_other = scatter_sum(act_part.reshape(2, 2, SEQ_LEN, pdim), x, c)
    act_seq = (act_own + swap(act_other, "x")).astype(bf16)

    out_blocks = out_part.reshape(2, 2, 2, SEQ_LEN, pdim)
    kept = lax.dynamic_index_in_dim(out_blocks, c, 2, False)
    given = lax.dynamic_index_in_dim(out_blocks, 1 - c, 2, False)
    kept = kept + swap(given, "c")
    own = lax.dynamic_index_in_dim(kept, x, 1, False)
    other = lax.dynamic_index_in_dim(kept, 1 - x, 1, False)
    out_seq = (own[0] + swap(other[0], "x") + swap(own[1], "y") + swap(other[1], ("y", "x"))).astype(bf16)

    proj_own = lax.dot_general(
        act_seq, out_seq, (((0,), (0,)), ((), ())), preferred_element_type=f32
    ).astype(bf16)
    gathered = [proj_own] + [
        lax.ppermute(proj_own, "z", [(i, (i + d) % depth) for i in range(depth)]) for d in range(1, depth)
    ]
    gathered = jnp.stack(gathered)
    if middle > 1:
        gathered = lax.all_gather(gathered, "m", axis=0, tiled=True)
    gathered = jnp.concatenate((gathered, swap(gathered, "x"), swap(gathered, "y"), swap(gathered, ("y", "x"))), 0)
    gathered = jnp.concatenate((gathered, swap(gathered, "c")), 0)
    seqs = gathered.shape[0]
    proj_grad = gathered.reshape(seqs, pdim * pdim)

    own_index = lax.axis_index(("z", "m", "y", "x", "c"))
    width = pdim * pdim // (depth * middle * 8)
    gram = lax.dot_general(
        test_matrix, test_matrix, (((0,), (0,)), ((), ())), preferred_element_type=f32
    )
    omega_sq = jnp.trace(gram)
    coeff_wide = jnp.dot(proj_grad, test_matrix, preferred_element_type=f32)
    coeff = coeff_wide.astype(bf16)
    overlap = dot_t(proj_grad, proj_grad)
    coeff_up = coeff.astype(f32)
    pairs = lax.dot_general(coeff_up, coeff_up, (((1,), (1,)), ((), ())), precision=lax.Precision.HIGHEST)
    square_sum = jnp.sum(overlap * pairs)
    core_sketch = lax.dot_general(
        coeff_wide, coeff_up, (((0,), (0,)), ((), ())), precision=lax.Precision.HIGHEST
    )
    own_rows = lax.dot_general(
        lax.dynamic_slice_in_dim(proj_grad, own_index * width, width, 1), coeff,
        (((0,), (0,)), ((), ())), preferred_element_type=f32,
    )
    shift = shift_scale * jnp.sqrt(square_sum / (omega_sq + tiny_value))
    core = core_sketch + shift * gram
    core = 0.5 * (core + core.T)
    lower = jnp.linalg.cholesky(core)
    omega_own = lax.dynamic_slice_in_dim(test_matrix, own_index * width, width, 0).astype(f32)
    shifted = own_rows + shift * omega_own
    return jax.scipy.linalg.solve_triangular(lower, shifted.T, lower=True).T


def solution(mesh):
    dp, tensor = mesh.shape["dp"], mesh.shape["tensor"]
    depth = math.gcd(dp // 2, LINE)
    grid = Mesh(
        mesh.devices.reshape(depth, dp // (2 * depth), 2, tensor // 2, 2), ("z", "m", "y", "x", "c")
    )
    dps, tensors = ("z", "m", "y"), ("x", "c")
    in_specs = (
        P(dps, tensors),
        P(dps, None),
        P(dps, tensors),
        P(dps, tensors),
        P(tensors, dps),
        P(None, tensors),
        P(None, tensors),
        P(),
    )
    out_specs = P(dps + tensors, None)
    return jax.shard_map(local, mesh=grid, in_specs=in_specs, out_specs=out_specs, check_vma=False)
```

```python
import functools

import jax
import jax.numpy as jnp
from jax import lax
from jax.experimental import pallas as pl
from jax.experimental.pallas import tpu as pltpu
from jax.sharding import Mesh, PartitionSpec as P

SEQ_LEN = 128
LINE = 4

shift_scale = 0.1
tiny_value = 1e-06

f32 = jnp.float32
bf16 = jnp.bfloat16


def swap(value, axis):
    if isinstance(axis, str):
        return lax.ppermute(value, axis, [(0, 1), (1, 0)])
    count = 2 ** len(axis)
    return lax.ppermute(value, axis, [(i, count - 1 - i) for i in range(count)])


def settle(*values):
    return lax.optimization_barrier(values)


def dot_t(left, right):
    return lax.dot_general(left, right, (((1,), (1,)), ((), ())), preferred_element_type=f32)


class Columns:
    def __init__(self, array, slots):
        self.arrays, self.slots = (array,), slots

    def copies(self, refs, table, k, chunk):
        start = pl.multiple_of(table[self.slots[k]] * chunk, chunk)
        return [(None, refs[0].at[:, pl.ds(start, chunk)])]


class Quarters:
    def __init__(self, arrays, slots):
        self.arrays, self.slots = arrays, slots

    def copies(self, refs, table, k, chunk):
        start = pl.multiple_of(table[self.slots[k] + 1] * chunk, chunk)
        place = table[self.slots[k]]
        return [(place == n, ref.at[:, pl.ds(start, chunk)]) for n, ref in enumerate(refs)]


class Rows:
    def __init__(self, array, part):
        self.array, self.part = array, part


def start_one(choices, target, sem):
    for flag, ref in choices:
        copy = pltpu.make_async_copy(ref, target, sem)
        if flag is None:
            copy.start()
        else:
            pl.when(flag)(copy.start)
    return copy


def stage_kernel(plan, table, *refs):
    tiles, pieces, rows, chunk, has_total, tails = plan
    refs = list(refs)
    sources = [[refs.pop(0) for _ in tile.arrays] for tile in tiles]
    blocks = [[refs.pop(0) for _ in piece] for piece, _ in pieces]
    total_in = refs.pop(0) if has_total else None
    if tails:
        tail_refs = [[refs.pop(0) for _ in range(n)] for n in tails]
        proj_in = refs.pop(0)
    out, grads, weights, total, sems = [refs.pop(0) for _ in range(5)]
    if tails:
        tail_vmem, proj_vmem, tail_sems = refs
    units = weights.shape[1]
    inner = table[0] == 1

    waits = []
    if has_total:
        copy = pltpu.make_async_copy(total_in, total, sems.at[len(pieces), 0])
        copy.start()
        waits.append(copy)
    copies = []
    for k, block in enumerate(blocks):
        mine = []
        if pieces[k][1] is not None:
            block = [block[0].at[pl.ds(pieces[k][1] * units, units), :]]
        choices = [(None, block[0])]
        if len(block) > 1:
            choices = [(inner, block[0]), (jnp.logical_not(inner), block[1])]
        mine.append(start_one(choices, weights.at[k], sems.at[k, len(tiles)]))
        for t, tile in enumerate(tiles):
            mine.append(start_one(tile.copies(sources[t], table, k, chunk), grads.at[k, t], sems.at[k, t]))
        copies.append(mine)
    tail_copies = []
    if tails:
        copy = pltpu.make_async_copy(
            proj_in.at[:, pl.ds(pl.multiple_of(table[1], 128), units)], proj_vmem, tail_sems.at[len(tails), 0]
        )
        copy.start()
        tail_copies.append(copy)
        for t, pair in enumerate(tail_refs):
            for which in range(2):
                ref = pair[which] if len(pair) == 2 else pair[0].at[which]
                copy = pltpu.make_async_copy(ref, tail_vmem.at[t, which], tail_sems.at[t, which])
                copy.start()
                tail_copies.append(copy)
    for copy in waits:
        copy.wait()
    goal = out if not tails else total
    for k in range(len(pieces)):
        for copy in copies[k]:
            copy.wait()
        for t in range(len(tiles)):
            term = dot_t(grads[k, t], weights[k])
            where = pl.ds(t * rows, rows)
            if k > 0:
                goal[where, :] += term
            elif has_total:
                goal[where, :] = total[where, :] + term
            else:
                goal[where, :] = term
    if tails:
        for copy in tail_copies:
            copy.wait()
        for t in range(len(tiles)):
            where = pl.ds(t * rows, rows)
            wide = tail_vmem[t, 1].astype(f32)
            logistic = jax.nn.sigmoid(wide)
            scaled = total[where, :] * tail_vmem[t, 0].astype(f32) * logistic * (1.0 + wide * (1.0 - logistic))
            out[where, :] = dot_t(scaled.astype(bf16), proj_vmem[...])


def stage(table, tiles, pieces, rows, total=None, tails=None, proj=None):
    parts = [p.part if isinstance(p, Rows) else None for p in pieces]
    pieces = [p.array if isinstance(p, Rows) else p for p in pieces]
    pieces = [p if isinstance(p, tuple) else (p,) for p in pieces]
    units, chunk = pieces[0][0].shape
    units = units if parts[0] is None else units // 2
    operands = [v for tile in tiles for v in tile.arrays] + [v for p in pieces for v in p]
    width = units
    if total is not None:
        operands.append(total)
    scratch = [
        pltpu.VMEM((len(pieces), len(tiles), rows, chunk), bf16),
        pltpu.VMEM((len(pieces), units, chunk), bf16),
        pltpu.VMEM((len(tiles) * rows, units) if total is not None else (8, 128), f32),
        pltpu.SemaphoreType.DMA((len(pieces) + 1, len(tiles) + 1)),
    ]
    if tails is not None:
        tails = [tail if isinstance(tail, tuple) else (tail,) for tail in tails]
        operands += [v for tail in tails for v in tail] + [proj]
        width = proj.shape[0]
        scratch += [
            pltpu.VMEM((len(tiles), 2, rows, units), bf16),
            pltpu.VMEM((width, units), bf16),
            pltpu.SemaphoreType.DMA((len(tails) + 1, 2)),
        ]
    plan = (tiles, list(zip(pieces, parts)), rows, chunk, total is not None, [len(tail) for tail in tails] if tails else None)
    height = len(tiles) * rows
    return pl.pallas_call(
        functools.partial(stage_kernel, plan),
        out_shape=jax.ShapeDtypeStruct((height, width), f32),
        in_specs=[pl.BlockSpec(memory_space=pltpu.SMEM)] + [pl.BlockSpec(memory_space=pl.ANY)] * len(operands),
        out_specs=pl.BlockSpec(memory_space=pltpu.VMEM),
        scratch_shapes=scratch,
        compiler_params=pltpu.CompilerParams(vmem_limit_bytes=44 * 2**20),
        cost_estimate=pl.CostEstimate(
            flops=2 * height * units * chunk * len(pieces),
            bytes_accessed=4 * height * units,
            transcendentals=0,
        ),
    )(table, *operands)


def local(tokens, grad_out, gate_pre, up_value, down_weight, in_proj, out_proj, test_matrix):
    z, y, x, c = (lax.axis_index(a) for a in ("z", "y", "x", "c"))
    middle = lax.axis_size("m")
    rows, width = grad_out.shape
    pdim = in_proj.shape[0]
    chunk = down_weight.shape[1] * middle
    if middle > 1:
        down_weight = lax.all_gather(down_weight, "m", axis=1, tiled=True)
        grad_out = grad_out.reshape(rows, LINE, middle, 2, -1).swapaxes(2, 3).reshape(rows, -1)
    half = down_weight.shape[0] // 2
    moved = half * 5 // 14 // 128 * 128
    stay = half - moved
    inner = (z > 0) & (z < LINE - 1)
    PAIR = [(0, 1), (1, 0), (2, 3), (3, 2)]
    IN, OUT, ACROSS = [(0, 1), (3, 2)], [(1, 0), (2, 3)], [(1, 2), (2, 1)]

    def along(value, pairs):
        return lax.ppermute(value, "z", pairs)

    def cut(value, index, dim, kept):
        start = index * half + (moved if kept else 0)
        return lax.dynamic_slice_in_dim(value, start, stay if kept else moved, dim)

    def both_values(index, kept):
        return jnp.stack((cut(up_value, index, 1, kept), cut(gate_pre, index, 1, kept)))

    quarter = width // 4
    k_own = cut(down_weight, y, 0, True)
    k_near, k_mid = along(k_own, PAIR), along(k_own, ACROSS)
    kt_own = swap(cut(down_weight, 1 - y, 0, True), "y")
    o_own, ot_send = cut(down_weight, y, 0, False), cut(down_weight, 1 - y, 0, False)
    sent = lax.dynamic_slice_in_dim(grad_out, (x * 2 + c) * quarter, quarter, 1)
    values_o, values_os = both_values(y, False), both_values(1 - y, False)
    k_own, k_near, k_mid, kt_own, o_own, ot_send, sent, values_o, values_os = settle(
        k_own, k_near, k_mid, kt_own, o_own, ot_send, sent, values_o, values_os
    )

    kt_near, kt_mid = along(kt_own, PAIR), along(kt_own, ACROSS)
    sent_y = swap(sent, "y")
    values_k, values_ks = both_values(y, True), both_values(1 - y, True)
    kt_near, kt_mid, sent_y, values_k, values_ks, sent, k_mid, k_near, ot_send = settle(
        kt_near, kt_mid, sent_y, values_k, values_ks, sent, k_mid, k_near, ot_send
    )

    grads_e, k_second, k_far = along(sent, IN), along(k_mid, OUT), along(k_near, ACROSS)
    ot_own = swap(ot_send, "y")
    sent_yx = swap(sent_y, "x")
    act_part = dot_t(tokens, in_proj)
    values_ks0 = swap(values_ks[0], "y")
    grads_e, k_second, k_far, ot_own, sent_y, sent_yx, act_part, kt_mid, kt_near, o_own = settle(
        grads_e, k_second, k_far, ot_own, sent_y, sent_yx, act_part, kt_mid, kt_near, o_own
    )

    o_both = jnp.concatenate((o_own, ot_own), 0)
    o_end, kt_second, kt_far = along(o_both, IN), along(kt_mid, OUT), along(kt_near, ACROSS)
    grads_ey = swap(grads_e, "y")
    grads_ex = swap(grads_e, "x")
    grads_y = (sent_y, swap(sent_y, "c"), sent_yx, swap(sent_yx, "c"))
    (o_end, kt_second, kt_far, grads_e, grads_ex, grads_ey, o_both, k_far, values_o, values_os, values_ks0, values_ks) = settle(
        o_end, kt_second, kt_far, grads_e, grads_ex, grads_ey, o_both, k_far, values_o, values_os, values_ks0, values_ks
    )

    values_e, k_third, o_mid = along(values_o, IN), along(k_far, OUT), along(o_both, ACROSS)
    values_oy = swap(values_os, "y")
    grads_eyx = swap(grads_ey, "x")
    grads_far = [(grads_e, swap(grads_e, "c"), grads_ex, swap(grads_ex, "c"))]

    own = x * 2 + c
    near = jnp.where(z % 2 == 0, z + 1, z - 1)
    other = jnp.where(z < 2, 2, 1)
    far = jnp.where(z < 2, 3, 0)

    def table(start, *chunks):
        values = [inner.astype(jnp.int32), start]
        for at, side in chunks:
            at = at * 2 + side
            values += [at, (at // 2) ^ own, at % 2]
        return jnp.stack([jnp.asarray(v, jnp.int32) for v in values])

    def slots(count, skip):
        return [2 + 3 * k + skip for k in range(count)]

    yt = 1 - y
    first = ((z, y), (z, yt), (near, y), (near, yt), (other, y), (other, yt))
    last = ((far, y), (far, yt))
    table_first = table(0, *first)

    def near_tiles(n):
        return [Columns(grad_out, slots(n, 0)), Quarters(grads_y, slots(n, 1))]

    def far_tiles(n):
        return [Quarters(arrays, slots(n, 1)) for arrays in grads_far]

    k_pieces = [k_own, kt_own, k_near, kt_near, (k_mid, k_second), (kt_mid, kt_second)]
    k_total = stage(table_first, near_tiles(6), k_pieces, rows)
    (values_e, k_third, o_mid, values_oy, grads_ey, grads_eyx, k_total, o_end, kt_far, values_ks) = settle(
        values_e, k_third, o_mid, values_oy, grads_ey, grads_eyx, k_total, o_end, kt_far, values_ks
    )

    values_ey, kt_third, o_far = along(values_oy, IN), along(kt_far, OUT), along(o_end, ACROSS)
    values_ks1 = swap(values_ks[1], "y")
    values_ky = (values_ks0, values_ks1)
    grads_far.append((grads_ey, swap(grads_ey, "c"), grads_eyx, swap(grads_eyx, "c")))
    o_total = stage(table_first, near_tiles(6) + far_tiles(6), [o_own, ot_own, Rows(o_end, 0), Rows(o_end, 1), Rows(o_mid, 0), Rows(o_mid, 1)], rows)
    o_total, values_ey, kt_third, o_far = settle(o_total, values_ey, kt_third, o_far)
    out_k = stage(
        table(y * half + moved, *last), near_tiles(2), [(k_far, k_third), (kt_far, kt_third)], rows, k_total,
        [values_k, values_ky], out_proj,
    )
    out_o = stage(
        table(y * half, *last), near_tiles(2) + far_tiles(2), [Rows(o_far, 0), Rows(o_far, 1)], rows, o_total,
        [values_o, values_oy, values_e, values_ey], out_proj,
    )

    act_blocks = act_part.reshape(2, 2, SEQ_LEN, pdim)
    act_kept = lax.dynamic_index_in_dim(act_blocks, c, 1, False) + swap(
        lax.dynamic_index_in_dim(act_blocks, 1 - c, 1, False), "c"
    )
    act_seq = (
        lax.dynamic_index_in_dim(act_kept, x, 0, False)
        + swap(lax.dynamic_index_in_dim(act_kept, 1 - x, 0, False), "x")
    ).astype(bf16)

    out_o = out_o.reshape(2, 2 * rows, pdim)
    blocks = jnp.stack((out_k + jnp.where(inner, out_o[0], 0.0), out_o[1])).reshape(2, 2, 2, 2, SEQ_LEN, pdim)
    kept = lax.dynamic_index_in_dim(blocks, c, 3, False) + swap(
        lax.dynamic_index_in_dim(blocks, 1 - c, 3, False), "c"
    )
    own_x = lax.dynamic_index_in_dim(kept, x, 2, False)
    other_x = lax.dynamic_index_in_dim(kept, 1 - x, 2, False)
    out_sum = own_x[:, 0] + swap(other_x[:, 0], "x") + swap(own_x[:, 1], "y") + swap(other_x[:, 1], ("y", "x"))
    out_seq = (out_sum[0] + lax.ppermute(out_sum[1], "z", [(1, 0), (2, 3)])).astype(bf16)

    proj_own = lax.dot_general(
        act_seq, out_seq, (((0,), (0,)), ((), ())), preferred_element_type=f32
    ).astype(bf16)
    gathered = [proj_own] + [
        lax.ppermute(proj_own, "z", [(i, (i + d) % LINE) for i in range(LINE)]) for d in range(1, LINE)
    ]
    gathered = jnp.stack(gathered)
    if middle > 1:
        gathered = lax.all_gather(gathered, "m", axis=0, tiled=True)
    gathered = jnp.concatenate((gathered, swap(gathered, "x"), swap(gathered, "y"), swap(gathered, ("y", "x"))), 0)
    gathered = jnp.concatenate((gathered, swap(gathered, "c")), 0)
    seqs = gathered.shape[0]
    proj_grad = gathered.reshape(seqs, pdim * pdim)

    own_index = lax.axis_index(("z", "m", "y", "x", "c"))
    own_width = pdim * pdim // (LINE * middle * 8)
    gram = lax.dot_general(
        test_matrix, test_matrix, (((0,), (0,)), ((), ())), preferred_element_type=f32
    )
    omega_sq = jnp.trace(gram)
    coeff_wide = jnp.dot(proj_grad, test_matrix, preferred_element_type=f32)
    coeff = coeff_wide.astype(bf16)
    overlap = dot_t(proj_grad, proj_grad)
    coeff_up = coeff.astype(f32)
    pairs = lax.dot_general(coeff_up, coeff_up, (((1,), (1,)), ((), ())), precision=lax.Precision.HIGHEST)
    square_sum = jnp.sum(overlap * pairs)
    core_sketch = lax.dot_general(
        coeff_wide, coeff_up, (((0,), (0,)), ((), ())), precision=lax.Precision.HIGHEST
    )
    own_rows = lax.dot_general(
        lax.dynamic_slice_in_dim(proj_grad, own_index * own_width, own_width, 1), coeff,
        (((0,), (0,)), ((), ())), preferred_element_type=f32,
    )
    shift = shift_scale * jnp.sqrt(square_sum / (omega_sq + tiny_value))
    core = core_sketch + shift * gram
    core = 0.5 * (core + core.T)
    lower = jnp.linalg.cholesky(core)
    omega_own = lax.dynamic_slice_in_dim(test_matrix, own_index * own_width, own_width, 0).astype(f32)
    shifted = own_rows + shift * omega_own
    return jax.scipy.linalg.solve_triangular(lower, shifted.T, lower=True).T


def solution(mesh):
    dp, tensor = mesh.shape["dp"], mesh.shape["tensor"]
    grid = Mesh(
        mesh.devices.reshape(LINE, dp // (2 * LINE), 2, tensor // 2, 2), ("z", "m", "y", "x", "c")
    )
    dps, tensors = ("z", "m", "y"), ("x", "c")
    in_specs = (
        P(dps, tensors),
        P(dps, None),
        P(dps, tensors),
        P(dps, tensors),
        P(tensors, dps),
        P(None, tensors),
        P(None, tensors),
        P(),
    )
    out_specs = P(dps + tensors, None)
    return jax.shard_map(local, mesh=grid, in_specs=in_specs, out_specs=out_specs, check_vma=False)
```

```python
import functools

import jax
import jax.numpy as jnp
from jax import lax
from jax.experimental import pallas as pl
from jax.experimental.pallas import tpu as pltpu
from jax.sharding import Mesh, PartitionSpec as P

SEQ_LEN = 128
LINE = 4

shift_scale = 0.1
tiny_value = 1e-06

f32 = jnp.float32
bf16 = jnp.bfloat16


def swap(value, axis):
    if isinstance(axis, str):
        return lax.ppermute(value, axis, [(0, 1), (1, 0)])
    count = 2 ** len(axis)
    return lax.ppermute(value, axis, [(i, count - 1 - i) for i in range(count)])


def settle(*values):
    return lax.optimization_barrier(values)


def dot_t(left, right):
    return lax.dot_general(left, right, (((1,), (1,)), ((), ())), preferred_element_type=f32)


class Columns:
    def __init__(self, array, slots):
        self.arrays, self.slots = (array,), slots

    def copies(self, refs, table, k, chunk):
        start = pl.multiple_of(table[self.slots[k]] * chunk, chunk)
        return [(None, refs[0].at[:, pl.ds(start, chunk)])]


class Quarters:
    def __init__(self, arrays, slots):
        self.arrays, self.slots = arrays, slots

    def copies(self, refs, table, k, chunk):
        start = pl.multiple_of(table[self.slots[k] + 1] * chunk, chunk)
        place = table[self.slots[k]]
        return [(place == n, ref.at[:, pl.ds(start, chunk)]) for n, ref in enumerate(refs)]


class Rows:
    def __init__(self, array, part):
        self.array, self.part = array, part


def start_one(choices, target, sem):
    for flag, ref in choices:
        copy = pltpu.make_async_copy(ref, target, sem)
        if flag is None:
            copy.start()
        else:
            pl.when(flag)(copy.start)
    return copy


def stage_kernel(plan, table, *refs):
    tiles, pieces, rows, chunk, has_total, tails = plan
    refs = list(refs)
    sources = [[refs.pop(0) for _ in tile.arrays] for tile in tiles]
    blocks = [[refs.pop(0) for _ in piece] for piece, _ in pieces]
    total_in = refs.pop(0) if has_total else None
    if tails:
        tail_refs = [[refs.pop(0) for _ in range(n)] for n in tails]
        proj_in = refs.pop(0)
    out, grads, weights, total, sems = [refs.pop(0) for _ in range(5)]
    if tails:
        tail_vmem, proj_vmem, tail_sems = refs
    units = weights.shape[1]
    inner = table[0] == 1

    waits = []
    if has_total:
        copy = pltpu.make_async_copy(total_in, total, sems.at[len(pieces), 0])
        copy.start()
        waits.append(copy)
    copies = []
    for k, block in enumerate(blocks):
        mine = []
        if pieces[k][1] is not None:
            block = [block[0].at[pl.ds(pieces[k][1] * units, units), :]]
        choices = [(None, block[0])]
        if len(block) > 1:
            choices = [(inner, block[0]), (jnp.logical_not(inner), block[1])]
        mine.append(start_one(choices, weights.at[k], sems.at[k, len(tiles)]))
        for t, tile in enumerate(tiles):
            mine.append(start_one(tile.copies(sources[t], table, k, chunk), grads.at[k, t], sems.at[k, t]))
        copies.append(mine)
    tail_copies = []
    if tails:
        copy = pltpu.make_async_copy(
            proj_in.at[:, pl.ds(pl.multiple_of(table[1], 128), units)], proj_vmem, tail_sems.at[len(tails), 0]
        )
        copy.start()
        tail_copies.append(copy)
        for t, pair in enumerate(tail_refs):
            for which in range(2):
                ref = pair[which] if len(pair) == 2 else pair[0].at[which]
                copy = pltpu.make_async_copy(ref, tail_vmem.at[t, which], tail_sems.at[t, which])
                copy.start()
                tail_copies.append(copy)
    for copy in waits:
        copy.wait()
    goal = out if not tails else total
    for k in range(len(pieces)):
        for copy in copies[k]:
            copy.wait()
        for t in range(len(tiles)):
            term = dot_t(grads[k, t], weights[k])
            where = pl.ds(t * rows, rows)
            if k > 0:
                goal[where, :] += term
            elif has_total:
                goal[where, :] = total[where, :] + term
            else:
                goal[where, :] = term
    if tails:
        for copy in tail_copies:
            copy.wait()
        for t in range(len(tiles)):
            where = pl.ds(t * rows, rows)
            wide = tail_vmem[t, 1].astype(f32)
            logistic = jax.nn.sigmoid(wide)
            scaled = total[where, :] * tail_vmem[t, 0].astype(f32) * logistic * (1.0 + wide * (1.0 - logistic))
            out[where, :] = dot_t(scaled.astype(bf16), proj_vmem[...])


def stage(table, tiles, pieces, rows, total=None, tails=None, proj=None):
    parts = [p.part if isinstance(p, Rows) else None for p in pieces]
    pieces = [p.array if isinstance(p, Rows) else p for p in pieces]
    pieces = [p if isinstance(p, tuple) else (p,) for p in pieces]
    units, chunk = pieces[0][0].shape
    units = units if parts[0] is None else units // 2
    operands = [v for tile in tiles for v in tile.arrays] + [v for p in pieces for v in p]
    width = units
    if total is not None:
        operands.append(total)
    scratch = [
        pltpu.VMEM((len(pieces), len(tiles), rows, chunk), bf16),
        pltpu.VMEM((len(pieces), units, chunk), bf16),
        pltpu.VMEM((len(tiles) * rows, units) if total is not None else (8, 128), f32),
        pltpu.SemaphoreType.DMA((len(pieces) + 1, len(tiles) + 1)),
    ]
    if tails is not None:
        tails = [tail if isinstance(tail, tuple) else (tail,) for tail in tails]
        operands += [v for tail in tails for v in tail] + [proj]
        width = proj.shape[0]
        scratch += [
            pltpu.VMEM((len(tiles), 2, rows, units), bf16),
            pltpu.VMEM((width, units), bf16),
            pltpu.SemaphoreType.DMA((len(tails) + 1, 2)),
        ]
    plan = (tiles, list(zip(pieces, parts)), rows, chunk, total is not None, [len(tail) for tail in tails] if tails else None)
    height = len(tiles) * rows
    return pl.pallas_call(
        functools.partial(stage_kernel, plan),
        out_shape=jax.ShapeDtypeStruct((height, width), f32),
        in_specs=[pl.BlockSpec(memory_space=pltpu.SMEM)] + [pl.BlockSpec(memory_space=pltpu.HBM)] * len(operands),
        out_specs=pl.BlockSpec(memory_space=pltpu.VMEM),
        scratch_shapes=scratch,
        compiler_params=pltpu.CompilerParams(vmem_limit_bytes=44 * 2**20),
        cost_estimate=pl.CostEstimate(
            flops=2 * height * units * chunk * len(pieces),
            bytes_accessed=4 * height * units,
            transcendentals=0,
        ),
    )(table, *operands)


def highest(left, right, dims):
    return lax.dot_general(
        left, right, (dims, ((), ())), precision=lax.Precision.HIGHEST, preferred_element_type=f32
    )


def inverse_factor(core, out):
    size, step = core.shape[0], 8
    shape = (step, size)
    lane = lax.broadcasted_iota(jnp.int32, shape, 1)
    row = lax.broadcasted_iota(jnp.int32, shape, 0)
    count = size // step
    left = [core[step * n : step * n + step, :] for n in range(count)]
    right = [jnp.where(lane == row + step * n, 1.0, 0.0) for n in range(count)]
    for b in range(count):
        columns = [
            {n: jnp.broadcast_to(left[n][:, step * b + j : step * b + j + 1], shape) for n in range(b, count)}
            for j in range(step)
        ]
        leads = [jnp.broadcast_to(left[b][j : j + 1, :], shape) for j in range(step)]
        twins = [jnp.broadcast_to(right[b][j : j + 1, :], shape) for j in range(step)]
        entry = [[jnp.broadcast_to(columns[j][b][i : i + 1, :], shape) for j in range(i + 1)] for i in range(step)]
        roots = []
        for k in range(step):
            pivot = entry[k][k]
            root = lax.rsqrt(pivot)
            root = root * (1.5 - 0.5 * pivot * root * root)
            roots.append(root)
            for i in range(k + 1, step):
                entry[i][k] = entry[i][k] * root
            for i in range(k + 1, step):
                for j in range(k + 1, i + 1):
                    entry[i][j] = entry[i][j] - entry[i][k] * entry[j][k]
        for k in range(step):
            leads[k], twins[k] = leads[k] * roots[k], twins[k] * roots[k]
            for j in range(k + 1, step):
                leads[j] = leads[j] - entry[j][k] * leads[k]
                twins[j] = twins[j] - entry[j][k] * twins[k]
        done = twins[0]
        for k in range(1, step):
            done = jnp.where(row == k, twins[k], done)
        out[step * b : step * b + step, :] = done
        for n in range(b + 1, count):
            for k in range(step):
                share = columns[k][n] * roots[k]
                for j in range(k + 1, step):
                    columns[j][n] = columns[j][n] - share * entry[j][k]
                left[n] = left[n] - share * leads[k]
                right[n] = right[n] - share * twins[k]


def factor_kernel(place, proj, omega, gram_in, out, inverse):
    rows = out.shape[0]
    wide = jnp.dot(proj[...], omega[...], preferred_element_type=f32)
    coeff = wide.astype(bf16)
    known = coeff.astype(f32)
    overlap = dot_t(proj[...], proj[...])
    square_sum = jnp.sum(overlap * highest(known, known, ((1,), (1,))), keepdims=True)
    gram = gram_in[...]
    diagonal = lax.broadcasted_iota(jnp.int32, gram.shape, 0) == lax.broadcasted_iota(jnp.int32, gram.shape, 1)
    omega_sq = jnp.sum(jnp.where(diagonal, gram, 0.0), keepdims=True)
    shift = shift_scale * jnp.sqrt(square_sum / (omega_sq + tiny_value))
    core = highest(wide, known, ((0,), (0,))) + shift * gram
    core = 0.5 * (core + core.T)
    inverse_factor(core, inverse)
    start = pl.multiple_of(place[0] * rows, rows)
    sketch = lax.dot_general(
        proj[:, pl.ds(start, rows)], coeff, (((0,), (0,)), ((), ())), preferred_element_type=f32
    )
    shifted = sketch + shift * omega[pl.ds(start, rows), :].astype(f32)
    out[...] = highest(shifted, inverse[...], ((1,), (1,)))


def factor_rows(proj_grad, test_matrix, gram, place, rows):
    rank_cols = test_matrix.shape[1]
    return pl.pallas_call(
        factor_kernel,
        out_shape=jax.ShapeDtypeStruct((rows, rank_cols), f32),
        in_specs=[pl.BlockSpec(memory_space=pltpu.SMEM)] + [pl.BlockSpec(memory_space=pltpu.VMEM)] * 3,
        out_specs=pl.BlockSpec(memory_space=pltpu.VMEM),
        scratch_shapes=[pltpu.VMEM((rank_cols, rank_cols), f32)],
        compiler_params=pltpu.CompilerParams(vmem_limit_bytes=32 * 2**20),
    )(place.astype(jnp.int32).reshape(1), proj_grad, test_matrix, gram)


def local(tokens, grad_out, gate_pre, up_value, down_weight, in_proj, out_proj, test_matrix):
    z, y, x, c = (lax.axis_index(a) for a in ("z", "y", "x", "c"))
    middle = lax.axis_size("m")
    rows, width = grad_out.shape
    pdim = in_proj.shape[0]
    chunk = down_weight.shape[1] * middle
    if middle > 1:
        down_weight = lax.all_gather(down_weight, "m", axis=1, tiled=True)
        grad_out = grad_out.reshape(rows, LINE, middle, 2, -1).swapaxes(2, 3).reshape(rows, -1)
    half = down_weight.shape[0] // 2
    moved = half * 5 // 14 // 128 * 128
    stay = half - moved
    inner = (z > 0) & (z < LINE - 1)
    PAIR = [(0, 1), (1, 0), (2, 3), (3, 2)]
    IN, OUT, ACROSS = [(0, 1), (3, 2)], [(1, 0), (2, 3)], [(1, 2), (2, 1)]

    def along(value, pairs):
        return lax.ppermute(value, "z", pairs)

    def cut(value, index, dim, kept):
        start = index * half + (moved if kept else 0)
        return lax.dynamic_slice_in_dim(value, start, stay if kept else moved, dim)

    def both_values(index, kept):
        return jnp.stack((cut(up_value, index, 1, kept), cut(gate_pre, index, 1, kept)))

    quarter = width // 4
    k_own = cut(down_weight, y, 0, True)
    k_near, k_mid = along(k_own, PAIR), along(k_own, ACROSS)
    kt_own = swap(cut(down_weight, 1 - y, 0, True), "y")
    o_own, ot_send = cut(down_weight, y, 0, False), cut(down_weight, 1 - y, 0, False)
    sent = lax.dynamic_slice_in_dim(grad_out, (x * 2 + c) * quarter, quarter, 1)
    values_o, values_os = both_values(y, False), both_values(1 - y, False)
    k_own, k_near, k_mid, kt_own, o_own, ot_send, sent, values_o, values_os = settle(
        k_own, k_near, k_mid, kt_own, o_own, ot_send, sent, values_o, values_os
    )

    kt_near, kt_mid = along(kt_own, PAIR), along(kt_own, ACROSS)
    sent_y = swap(sent, "y")
    values_k, values_ks = both_values(y, True), both_values(1 - y, True)
    gram = lax.dot_general(
        test_matrix, test_matrix, (((0,), (0,)), ((), ())), preferred_element_type=f32
    )
    kt_near, kt_mid, sent_y, values_k, values_ks, sent, k_mid, k_near, ot_send, gram = settle(
        kt_near, kt_mid, sent_y, values_k, values_ks, sent, k_mid, k_near, ot_send, gram
    )

    grads_e, k_second, k_far = along(sent, IN), along(k_mid, OUT), along(k_near, ACROSS)
    ot_own = swap(ot_send, "y")
    sent_yx = swap(sent_y, "x")
    act_part = dot_t(tokens, in_proj)
    values_ks0 = swap(values_ks[0], "y")
    grads_e, k_second, k_far, ot_own, sent_y, sent_yx, act_part, kt_mid, kt_near, o_own = settle(
        grads_e, k_second, k_far, ot_own, sent_y, sent_yx, act_part, kt_mid, kt_near, o_own
    )

    o_both = jnp.concatenate((o_own, ot_own), 0)
    o_end, kt_second, kt_far = along(o_both, IN), along(kt_mid, OUT), along(kt_near, ACROSS)
    grads_ey = swap(grads_e, "y")
    grads_ex = swap(grads_e, "x")
    grads_y = (sent_y, swap(sent_y, "c"), sent_yx, swap(sent_yx, "c"))
    (o_end, kt_second, kt_far, grads_e, grads_ex, grads_ey, o_both, k_far, values_o, values_os, values_ks0, values_ks) = settle(
        o_end, kt_second, kt_far, grads_e, grads_ex, grads_ey, o_both, k_far, values_o, values_os, values_ks0, values_ks
    )

    values_e, k_third, o_mid = along(values_o, IN), along(k_far, OUT), along(o_both, ACROSS)
    values_oy = swap(values_os, "y")
    grads_eyx = swap(grads_ey, "x")
    grads_far = [(grads_e, swap(grads_e, "c"), grads_ex, swap(grads_ex, "c"))]

    own = x * 2 + c
    near = jnp.where(z % 2 == 0, z + 1, z - 1)
    other = jnp.where(z < 2, 2, 1)
    far = jnp.where(z < 2, 3, 0)

    def table(start, *chunks):
        values = [inner.astype(jnp.int32), start]
        for at, side in chunks:
            at = at * 2 + side
            values += [at, (at // 2) ^ own, at % 2]
        return jnp.stack([jnp.asarray(v, jnp.int32) for v in values])

    def slots(count, skip):
        return [2 + 3 * k + skip for k in range(count)]

    yt = 1 - y
    first = ((z, y), (z, yt), (near, y), (near, yt), (other, y), (other, yt))
    last = ((far, y), (far, yt))
    table_first = table(0, *first)

    def near_tiles(n):
        return [Columns(grad_out, slots(n, 0)), Quarters(grads_y, slots(n, 1))]

    def far_tiles(n):
        return [Quarters(arrays, slots(n, 1)) for arrays in grads_far]

    k_pieces = [k_own, kt_own, k_near, kt_near, (k_mid, k_second), (kt_mid, kt_second)]
    k_total = stage(table_first, near_tiles(6), k_pieces, rows)
    (values_e, k_third, o_mid, values_oy, grads_ey, grads_eyx, k_total, o_end, kt_far, values_ks) = settle(
        values_e, k_third, o_mid, values_oy, grads_ey, grads_eyx, k_total, o_end, kt_far, values_ks
    )

    values_ey, kt_third, o_far = along(values_oy, IN), along(kt_far, OUT), along(o_end, ACROSS)
    values_ks1 = swap(values_ks[1], "y")
    values_ky = (values_ks0, values_ks1)
    grads_far.append((grads_ey, swap(grads_ey, "c"), grads_eyx, swap(grads_eyx, "c")))
    o_total = stage(table_first, near_tiles(6) + far_tiles(6), [o_own, ot_own, Rows(o_end, 0), Rows(o_end, 1), Rows(o_mid, 0), Rows(o_mid, 1)], rows)
    o_total, values_ey, kt_third, o_far = settle(o_total, values_ey, kt_third, o_far)
    out_k = stage(
        table(y * half + moved, *last), near_tiles(2), [(k_far, k_third), (kt_far, kt_third)], rows, k_total,
        [values_k, values_ky], out_proj,
    )
    out_o = stage(
        table(y * half, *last), near_tiles(2) + far_tiles(2), [Rows(o_far, 0), Rows(o_far, 1)], rows, o_total,
        [values_o, values_oy, values_e, values_ey], out_proj,
    )

    act_blocks = act_part.reshape(2, 2, SEQ_LEN, pdim)
    act_kept = lax.dynamic_index_in_dim(act_blocks, c, 1, False) + swap(
        lax.dynamic_index_in_dim(act_blocks, 1 - c, 1, False), "c"
    )
    act_seq = (
        lax.dynamic_index_in_dim(act_kept, x, 0, False)
        + swap(lax.dynamic_index_in_dim(act_kept, 1 - x, 0, False), "x")
    ).astype(bf16)

    out_o = out_o.reshape(2, 2 * rows, pdim)
    blocks = jnp.stack((out_k + jnp.where(inner, out_o[0], 0.0), out_o[1])).reshape(2, 2, 2, 2, SEQ_LEN, pdim)
    kept = lax.dynamic_index_in_dim(blocks, c, 3, False) + swap(
        lax.dynamic_index_in_dim(blocks, 1 - c, 3, False), "c"
    )
    own_x = lax.dynamic_index_in_dim(kept, x, 2, False)
    other_x = lax.dynamic_index_in_dim(kept, 1 - x, 2, False)
    out_sum = own_x[:, 0] + swap(other_x[:, 0], "x") + swap(own_x[:, 1], "y") + swap(other_x[:, 1], ("y", "x"))
    out_seq = (out_sum[0] + lax.ppermute(out_sum[1], "z", [(1, 0), (2, 3)])).astype(bf16)

    proj_own = lax.dot_general(
        act_seq, out_seq, (((0,), (0,)), ((), ())), preferred_element_type=f32
    ).astype(bf16)
    gathered = [proj_own] + [
        lax.ppermute(proj_own, "z", [(i, (i + d) % LINE) for i in range(LINE)]) for d in range(1, LINE)
    ]
    gathered = jnp.stack(gathered)
    if middle > 1:
        gathered = lax.all_gather(gathered, "m", axis=0, tiled=True)
    gathered = jnp.concatenate((gathered, swap(gathered, "x"), swap(gathered, "y"), swap(gathered, ("y", "x"))), 0)
    gathered = jnp.concatenate((gathered, swap(gathered, "c")), 0)
    seqs = gathered.shape[0]
    proj_grad = gathered.reshape(seqs, pdim * pdim)

    own_index = lax.axis_index(("z", "m", "y", "x", "c"))
    own_width = pdim * pdim // (LINE * middle * 8)
    return factor_rows(proj_grad, test_matrix, gram, own_index, own_width)


def solution(mesh):
    dp, tensor = mesh.shape["dp"], mesh.shape["tensor"]
    grid = Mesh(
        mesh.devices.reshape(LINE, dp // (2 * LINE), 2, tensor // 2, 2), ("z", "m", "y", "x", "c")
    )
    dps, tensors = ("z", "m", "y"), ("x", "c")
    in_specs = (
        P(dps, tensors),
        P(dps, None),
        P(dps, tensors),
        P(dps, tensors),
        P(tensors, dps),
        P(None, tensors),
        P(None, tensors),
        P(),
    )
    out_specs = P(dps + tensors, None)
    return jax.shard_map(local, mesh=grid, in_specs=in_specs, out_specs=out_specs, check_vma=False)
```

```python
import functools

import jax
import jax.numpy as jnp
from jax import lax
from jax.experimental import pallas as pl
from jax.experimental.pallas import tpu as pltpu
from jax.sharding import Mesh, PartitionSpec as P

SEQ_LEN = 128
LINE = 4

shift_scale = 0.1
tiny_value = 1e-06

f32 = jnp.float32
bf16 = jnp.bfloat16


def swap(value, axis):
    if isinstance(axis, str):
        return lax.ppermute(value, axis, [(0, 1), (1, 0)])
    count = 2 ** len(axis)
    return lax.ppermute(value, axis, [(i, count - 1 - i) for i in range(count)])


def settle(*values):
    return lax.optimization_barrier(values)


def dot_t(left, right):
    return lax.dot_general(left, right, (((1,), (1,)), ((), ())), preferred_element_type=f32)


class Columns:
    def __init__(self, array, slots):
        self.arrays, self.slots = (array,), slots

    def copies(self, refs, table, k, chunk):
        start = pl.multiple_of(table[self.slots[k]] * chunk, chunk)
        return [(None, refs[0].at[:, pl.ds(start, chunk)])]


class Quarters:
    def __init__(self, arrays, slots):
        self.arrays, self.slots = arrays, slots

    def copies(self, refs, table, k, chunk):
        start = pl.multiple_of(table[self.slots[k] + 1] * chunk, chunk)
        place = table[self.slots[k]]
        return [(place == n, ref.at[:, pl.ds(start, chunk)]) for n, ref in enumerate(refs)]


class Rows:
    def __init__(self, array, part):
        self.array, self.part = array, part


def start_one(choices, target, sem):
    for flag, ref in choices:
        copy = pltpu.make_async_copy(ref, target, sem)
        if flag is None:
            copy.start()
        else:
            pl.when(flag)(copy.start)
    return copy


def stage_kernel(plan, table, *refs):
    tiles, pieces, rows, chunk, has_total, tails = plan
    refs = list(refs)
    sources = [[refs.pop(0) for _ in tile.arrays] for tile in tiles]
    blocks = [[refs.pop(0) for _ in piece] for piece, _ in pieces]
    total_in = refs.pop(0) if has_total else None
    if tails:
        tail_refs = [[refs.pop(0) for _ in range(n)] for n in tails]
        proj_in = refs.pop(0)
    out, grads, weights, total, sems = [refs.pop(0) for _ in range(5)]
    if tails:
        tail_vmem, proj_vmem, tail_sems = refs
    units = weights.shape[1]
    inner = table[0] == 1

    def start_total(t):
        where = pl.ds(t * rows, rows)
        return start_one([(None, total_in.at[where, :])], total.at[where, :], sems.at[len(pieces), t])

    def start_grads(k, t):
        return start_one(tiles[t].copies(sources[t], table, k, chunk), grads.at[k, t], sems.at[k, t])

    def start_piece(k):
        block = blocks[k]
        if pieces[k][1] is not None:
            block = [block[0].at[pl.ds(pieces[k][1] * units, units), :]]
        choices = [(None, block[0])]
        if len(block) > 1:
            choices = [(inner, block[0]), (jnp.logical_not(inner), block[1])]
        return start_one(choices, weights.at[k], sems.at[k, len(tiles)])

    if not tails:
        copies = [[start_piece(k)] + [start_grads(k, t) for t in range(len(tiles))] for k in range(len(pieces))]
        for k in range(len(pieces)):
            for copy in copies[k]:
                copy.wait()
            for t in range(len(tiles)):
                term = dot_t(grads[k, t], weights[k])
                where = pl.ds(t * rows, rows)
                if k > 0:
                    out[where, :] += term
                else:
                    out[where, :] = term
        return

    shared = [start_piece(k) for k in range(len(pieces))]
    shared.append(
        start_one(
            [(None, proj_in.at[:, pl.ds(pl.multiple_of(table[1], 128), units)])], proj_vmem, tail_sems.at[len(tails), 0]
        )
    )
    copies = []
    for t, pair in enumerate(tail_refs):
        mine = [start_grads(k, t) for k in range(len(pieces))] + [start_total(t)]
        for which in range(2):
            ref = pair[which] if len(pair) == 2 else pair[0].at[which]
            mine.append(start_one([(None, ref)], tail_vmem.at[t, which], tail_sems.at[t, which]))
        copies.append(mine)
    for copy in shared:
        copy.wait()
    for t in range(len(tiles)):
        for copy in copies[t]:
            copy.wait()
        where = pl.ds(t * rows, rows)
        value = total[where, :]
        for k in range(len(pieces)):
            value = value + dot_t(grads[k, t], weights[k])
        wide = tail_vmem[t, 1].astype(f32)
        logistic = 0.5 + 0.5 * jnp.tanh(0.5 * wide)
        scaled = value * tail_vmem[t, 0].astype(f32) * logistic * (1.0 + wide * (1.0 - logistic))
        out[where, :] = dot_t(scaled.astype(bf16), proj_vmem[...])


def stage(table, tiles, pieces, rows, total=None, tails=None, proj=None):
    parts = [p.part if isinstance(p, Rows) else None for p in pieces]
    pieces = [p.array if isinstance(p, Rows) else p for p in pieces]
    pieces = [p if isinstance(p, tuple) else (p,) for p in pieces]
    units, chunk = pieces[0][0].shape
    units = units if parts[0] is None else units // 2
    operands = [v for tile in tiles for v in tile.arrays] + [v for p in pieces for v in p]
    width = units
    if total is not None:
        operands.append(total)
    scratch = [
        pltpu.VMEM((len(pieces), len(tiles), rows, chunk), bf16),
        pltpu.VMEM((len(pieces), units, chunk), bf16),
        pltpu.VMEM((len(tiles) * rows, units) if total is not None else (8, 128), f32),
        pltpu.SemaphoreType.DMA((len(pieces) + 1, len(tiles) + 1)),
    ]
    if tails is not None:
        tails = [tail if isinstance(tail, tuple) else (tail,) for tail in tails]
        operands += [v for tail in tails for v in tail] + [proj]
        width = proj.shape[0]
        scratch += [
            pltpu.VMEM((len(tiles), 2, rows, units), bf16),
            pltpu.VMEM((width, units), bf16),
            pltpu.SemaphoreType.DMA((len(tails) + 1, 2)),
        ]
    plan = (tiles, list(zip(pieces, parts)), rows, chunk, total is not None, [len(tail) for tail in tails] if tails else None)
    height = len(tiles) * rows
    return pl.pallas_call(
        functools.partial(stage_kernel, plan),
        out_shape=jax.ShapeDtypeStruct((height, width), f32),
        in_specs=[pl.BlockSpec(memory_space=pltpu.SMEM)] + [pl.BlockSpec(memory_space=pltpu.HBM)] * len(operands),
        out_specs=pl.BlockSpec(memory_space=pltpu.VMEM),
        scratch_shapes=scratch,
        compiler_params=pltpu.CompilerParams(vmem_limit_bytes=44 * 2**20),
        cost_estimate=pl.CostEstimate(
            flops=0,
            bytes_accessed=0,
            transcendentals=0,
        ),
    )(table, *operands)


def highest(left, right, dims):
    return lax.dot_general(
        left, right, (dims, ((), ())), precision=lax.Precision.HIGHEST, preferred_element_type=f32
    )


def inverse_factor(core, out):
    size, step = core.shape[0], 8
    shape = (step, size)
    lane = lax.broadcasted_iota(jnp.int32, shape, 1)
    row = lax.broadcasted_iota(jnp.int32, shape, 0)
    count = size // step
    left = [core[step * n : step * n + step, :] for n in range(count)]
    right = [jnp.where(lane == row + step * n, 1.0, 0.0) for n in range(count)]
    for b in range(count):
        columns = [
            {n: jnp.broadcast_to(left[n][:, step * b + j : step * b + j + 1], shape) for n in range(b, count)}
            for j in range(step)
        ]
        leads = [jnp.broadcast_to(left[b][j : j + 1, :], shape) for j in range(step)]
        twins = [jnp.broadcast_to(right[b][j : j + 1, :], shape) for j in range(step)]
        entry = [[jnp.broadcast_to(columns[j][b][i : i + 1, :], shape) for j in range(i + 1)] for i in range(step)]
        roots = []
        for k in range(step):
            pivot = entry[k][k]
            root = lax.rsqrt(pivot)
            root = root * (1.5 - 0.5 * pivot * root * root)
            roots.append(root)
            for i in range(k + 1, step):
                entry[i][k] = entry[i][k] * root
            for i in range(k + 1, step):
                for j in range(k + 1, i + 1):
                    entry[i][j] = entry[i][j] - entry[i][k] * entry[j][k]
        for k in range(step):
            leads[k], twins[k] = leads[k] * roots[k], twins[k] * roots[k]
            for j in range(k + 1, step):
                leads[j] = leads[j] - entry[j][k] * leads[k]
                twins[j] = twins[j] - entry[j][k] * twins[k]
        done = twins[0]
        for k in range(1, step):
            done = jnp.where(row == k, twins[k], done)
        out[step * b : step * b + step, :] = done
        for n in range(b + 1, count):
            for k in range(step):
                share = columns[k][n] * roots[k]
                for j in range(k + 1, step):
                    columns[j][n] = columns[j][n] - share * entry[j][k]
                left[n] = left[n] - share * leads[k]
                right[n] = right[n] - share * twins[k]


def factor_kernel(place, proj, omega_in, gram_in, out, inverse, omega, sems):
    rows = out.shape[0]
    parts = sems.shape[0]
    length = omega.shape[0] // parts
    spans = [pl.ds(n * length, length) for n in range(parts)]
    copies = [pltpu.make_async_copy(omega_in.at[span, :], omega.at[span, :], sems.at[n]) for n, span in enumerate(spans)]
    for copy in copies:
        copy.start()
    overlap = dot_t(proj[...], proj[...])
    wide = 0.0
    for copy, span in zip(copies, spans):
        copy.wait()
        wide = wide + jnp.dot(proj[:, span], omega[span, :], preferred_element_type=f32)
    coeff = wide.astype(bf16)
    known = coeff.astype(f32)
    square_sum = jnp.sum(overlap * highest(known, known, ((1,), (1,))), keepdims=True)
    gram = gram_in[...]
    diagonal = lax.broadcasted_iota(jnp.int32, gram.shape, 0) == lax.broadcasted_iota(jnp.int32, gram.shape, 1)
    omega_sq = jnp.sum(jnp.where(diagonal, gram, 0.0), keepdims=True)
    shift = shift_scale * jnp.sqrt(square_sum / (omega_sq + tiny_value))
    core = highest(wide, known, ((0,), (0,))) + shift * gram
    core = 0.5 * (core + core.T)
    inverse_factor(core, inverse)
    start = pl.multiple_of(place[0] * rows, rows)
    sketch = lax.dot_general(
        proj[:, pl.ds(start, rows)], coeff, (((0,), (0,)), ((), ())), preferred_element_type=f32
    )
    shifted = sketch + shift * omega[pl.ds(start, rows), :].astype(f32)
    out[...] = highest(shifted, inverse[...], ((1,), (1,)))


def factor_rows(proj_grad, test_matrix, gram, place, rows):
    rank_cols = test_matrix.shape[1]
    return pl.pallas_call(
        factor_kernel,
        out_shape=jax.ShapeDtypeStruct((rows, rank_cols), f32),
        in_specs=[
            pl.BlockSpec(memory_space=pltpu.SMEM),
            pl.BlockSpec(memory_space=pltpu.VMEM),
            pl.BlockSpec(memory_space=pltpu.HBM),
            pl.BlockSpec(memory_space=pltpu.VMEM),
        ],
        out_specs=pl.BlockSpec(memory_space=pltpu.VMEM),
        scratch_shapes=[
            pltpu.VMEM((rank_cols, rank_cols), f32),
            pltpu.VMEM(test_matrix.shape, bf16),
            pltpu.SemaphoreType.DMA((4,)),
        ],
        compiler_params=pltpu.CompilerParams(vmem_limit_bytes=32 * 2**20),
    )(place.astype(jnp.int32).reshape(1), proj_grad, test_matrix, gram)


def local(tokens, grad_out, gate_pre, up_value, down_weight, in_proj, out_proj, test_matrix):
    z, y, x, c = (lax.axis_index(a) for a in ("z", "y", "x", "c"))
    middle = lax.axis_size("m")
    rows, width = grad_out.shape
    pdim = in_proj.shape[0]
    chunk = down_weight.shape[1] * middle
    if middle > 1:
        down_weight = lax.all_gather(down_weight, "m", axis=1, tiled=True)
        grad_out = grad_out.reshape(rows, LINE, middle, 2, -1).swapaxes(2, 3).reshape(rows, -1)
    half = down_weight.shape[0] // 2
    moved = half * 5 // 14 // 128 * 128
    stay = half - moved
    inner = (z > 0) & (z < LINE - 1)
    PAIR = [(0, 1), (1, 0), (2, 3), (3, 2)]
    IN, OUT, ACROSS = [(0, 1), (3, 2)], [(1, 0), (2, 3)], [(1, 2), (2, 1)]

    def along(value, pairs):
        return lax.ppermute(value, "z", pairs)

    def cut(value, index, dim, kept):
        start = index * half + (moved if kept else 0)
        return lax.dynamic_slice_in_dim(value, start, stay if kept else moved, dim)

    def both_values(index, kept):
        return jnp.stack((cut(up_value, index, 1, kept), cut(gate_pre, index, 1, kept)))

    quarter = width // 4
    k_own = cut(down_weight, y, 0, True)
    k_near, k_mid = along(k_own, PAIR), along(k_own, ACROSS)
    kt_own = swap(cut(down_weight, 1 - y, 0, True), "y")
    o_own, ot_send = cut(down_weight, y, 0, False), cut(down_weight, 1 - y, 0, False)
    sent = lax.dynamic_slice_in_dim(grad_out, (x * 2 + c) * quarter, quarter, 1)
    values_o, values_os = both_values(y, False), both_values(1 - y, False)
    k_own, k_near, k_mid, kt_own, o_own, ot_send, sent, values_o, values_os = settle(
        k_own, k_near, k_mid, kt_own, o_own, ot_send, sent, values_o, values_os
    )

    kt_near, kt_mid = along(kt_own, PAIR), along(kt_own, ACROSS)
    sent_y = swap(sent, "y")
    values_k, values_ks = both_values(y, True), both_values(1 - y, True)
    gram = lax.dot_general(
        test_matrix, test_matrix, (((0,), (0,)), ((), ())), preferred_element_type=f32
    )
    kt_near, kt_mid, sent_y, values_k, values_ks, sent, k_mid, k_near, ot_send, gram = settle(
        kt_near, kt_mid, sent_y, values_k, values_ks, sent, k_mid, k_near, ot_send, gram
    )

    grads_e, k_second, k_far = along(sent, IN), along(k_mid, OUT), along(k_near, ACROSS)
    ot_own = swap(ot_send, "y")
    sent_yx = swap(sent_y, "x")
    act_part = dot_t(tokens, in_proj)
    values_ks0 = swap(values_ks[0], "y")
    grads_e, k_second, k_far, ot_own, sent_y, sent_yx, act_part, kt_mid, kt_near, o_own = settle(
        grads_e, k_second, k_far, ot_own, sent_y, sent_yx, act_part, kt_mid, kt_near, o_own
    )

    o_both = jnp.concatenate((o_own, ot_own), 0)
    o_end, kt_second, kt_far = along(o_both, IN), along(kt_mid, OUT), along(kt_near, ACROSS)
    grads_ey = swap(grads_e, "y")
    grads_ex = swap(grads_e, "x")
    grads_y = (sent_y, swap(sent_y, "c"), sent_yx, swap(sent_yx, "c"))
    (o_end, kt_second, kt_far, grads_e, grads_ex, grads_ey, o_both, k_far, values_o, values_os, values_ks0, values_ks) = settle(
        o_end, kt_second, kt_far, grads_e, grads_ex, grads_ey, o_both, k_far, values_o, values_os, values_ks0, values_ks
    )

    values_e, k_third, o_mid = along(values_o, IN), along(k_far, OUT), along(o_both, ACROSS)
    values_oy = swap(values_os, "y")
    grads_eyx = swap(grads_ey, "x")
    own = x * 2 + c
    near = jnp.where(z % 2 == 0, z + 1, z - 1)
    other = jnp.where(z < 2, 2, 1)
    far = jnp.where(z < 2, 3, 0)

    def table(start, *chunks):
        values = [inner.astype(jnp.int32), start]
        for at, side in chunks:
            at = at * 2 + side
            values += [at, (at // 2) ^ own, at % 2]
        return jnp.stack([jnp.asarray(v, jnp.int32) for v in values])

    def slots(count, skip):
        return [2 + 3 * k + skip for k in range(count)]

    yt = 1 - y
    first = ((z, y), (z, yt), (near, y), (near, yt), (other, y), (other, yt))
    last = ((far, y), (far, yt))
    table_first = table(0, *first)

    def near_tiles(n):
        return [Columns(grad_out, slots(n, 0)), Quarters(grads_y, slots(n, 1))]

    def far_tiles(n):
        return [Quarters(arrays, slots(n, 1)) for arrays in grads_far]

    k_pieces = [k_own, kt_own, k_near, kt_near, (k_mid, k_second), (kt_mid, kt_second)]
    k_total = stage(table_first, near_tiles(6), k_pieces, rows)
    k_total, grads_e, grads_ex = settle(k_total, grads_e, grads_ex)
    grads_far = [(grads_e, swap(grads_e, "c"), grads_ex, swap(grads_ex, "c"))]
    (values_e, k_third, o_mid, values_oy, grads_ey, grads_eyx, k_total, o_end, kt_far, values_ks) = settle(
        values_e, k_third, o_mid, values_oy, grads_ey, grads_eyx, k_total, o_end, kt_far, values_ks
    )

    values_ey, kt_third, o_far = along(values_oy, IN), along(kt_far, OUT), along(o_end, ACROSS)
    values_ks1 = swap(values_ks[1], "y")
    values_ky = (values_ks0, values_ks1)
    grads_far.append((grads_ey, swap(grads_ey, "c"), grads_eyx, swap(grads_eyx, "c")))
    o_total = stage(table_first, near_tiles(6) + far_tiles(6), [o_own, ot_own, Rows(o_end, 0), Rows(o_end, 1), Rows(o_mid, 0), Rows(o_mid, 1)], rows)
    o_total, values_ey, kt_third, o_far = settle(o_total, values_ey, kt_third, o_far)
    out_k = stage(
        table(y * half + moved, *last), near_tiles(2), [(k_far, k_third), (kt_far, kt_third)], rows, k_total,
        [values_k, values_ky], out_proj,
    )
    out_o = stage(
        table(y * half, *last), near_tiles(2) + far_tiles(2), [Rows(o_far, 0), Rows(o_far, 1)], rows, o_total,
        [values_o, values_oy, values_e, values_ey], out_proj,
    )

    act_blocks = act_part.reshape(2, 2, SEQ_LEN, pdim)
    act_kept = lax.dynamic_index_in_dim(act_blocks, c, 1, False) + swap(
        lax.dynamic_index_in_dim(act_blocks, 1 - c, 1, False), "c"
    )
    act_seq = (
        lax.dynamic_index_in_dim(act_kept, x, 0, False)
        + swap(lax.dynamic_index_in_dim(act_kept, 1 - x, 0, False), "x")
    ).astype(bf16)

    out_o = out_o.reshape(2, 2 * rows, pdim)
    blocks = jnp.stack((out_k + jnp.where(inner, out_o[0], 0.0), out_o[1])).reshape(2, 2, 2, 2, SEQ_LEN, pdim)
    kept = lax.dynamic_index_in_dim(blocks, c, 3, False) + swap(
        lax.dynamic_index_in_dim(blocks, 1 - c, 3, False), "c"
    )
    own_x = lax.dynamic_index_in_dim(kept, x, 2, False)
    other_x = lax.dynamic_index_in_dim(kept, 1 - x, 2, False)
    out_sum = own_x[:, 0] + swap(other_x[:, 0], "x") + swap(own_x[:, 1], "y") + swap(other_x[:, 1], ("y", "x"))
    out_seq = (out_sum[0] + lax.ppermute(out_sum[1], "z", [(1, 0), (2, 3)])).astype(bf16)

    proj_own = lax.dot_general(
        act_seq, out_seq, (((0,), (0,)), ((), ())), preferred_element_type=f32
    ).astype(bf16)
    gathered = [proj_own] + [
        lax.ppermute(proj_own, "z", [(i, (i + d) % LINE) for i in range(LINE)]) for d in range(1, LINE)
    ]
    gathered = jnp.stack(gathered)
    if middle > 1:
        gathered = lax.all_gather(gathered, "m", axis=0, tiled=True)
    gathered = jnp.concatenate((gathered, swap(gathered, "x"), swap(gathered, "y"), swap(gathered, ("y", "x"))), 0)
    gathered = jnp.concatenate((gathered, swap(gathered, "c")), 0)
    seqs = gathered.shape[0]
    proj_grad = gathered.reshape(seqs, pdim * pdim)

    own_index = lax.axis_index(("z", "m", "y", "x", "c"))
    own_width = pdim * pdim // (LINE * middle * 8)
    return factor_rows(proj_grad, test_matrix, gram, own_index, own_width)


def solution(mesh):
    dp, tensor = mesh.shape["dp"], mesh.shape["tensor"]
    grid = Mesh(
        mesh.devices.reshape(LINE, dp // (2 * LINE), 2, tensor // 2, 2), ("z", "m", "y", "x", "c")
    )
    dps, tensors = ("z", "m", "y"), ("x", "c")
    in_specs = (
        P(dps, tensors),
        P(dps, None),
        P(dps, tensors),
        P(dps, tensors),
        P(tensors, dps),
        P(None, tensors),
        P(None, tensors),
        P(),
    )
    out_specs = P(dps + tensors, None)
    return jax.shard_map(local, mesh=grid, in_specs=in_specs, out_specs=out_specs, check_vma=False)
```

```python
import functools

import jax
import jax.numpy as jnp
from jax import lax
from jax.experimental import pallas as pl
from jax.experimental.pallas import tpu as pltpu
from jax.sharding import Mesh, PartitionSpec as P

SEQ_LEN = 128
LINE = 4

shift_scale = 0.1
tiny_value = 1e-06

f32 = jnp.float32
bf16 = jnp.bfloat16


def swap(value, axis):
    if isinstance(axis, str):
        return lax.ppermute(value, axis, [(0, 1), (1, 0)])
    count = 2 ** len(axis)
    return lax.ppermute(value, axis, [(i, count - 1 - i) for i in range(count)])


def settle(*values):
    return lax.optimization_barrier(values)


def dot_t(left, right):
    return lax.dot_general(left, right, (((1,), (1,)), ((), ())), preferred_element_type=f32)


class Columns:
    def __init__(self, array, slots):
        self.arrays, self.slots = (array,), slots

    def copies(self, refs, table, k, chunk):
        start = pl.multiple_of(table[self.slots[k]] * chunk, chunk)
        return [(None, refs[0].at[:, pl.ds(start, chunk)])]


class Quarters:
    def __init__(self, arrays, slots):
        self.arrays, self.slots = arrays, slots

    def copies(self, refs, table, k, chunk):
        start = pl.multiple_of(table[self.slots[k] + 1] * chunk, chunk)
        place = table[self.slots[k]]
        return [(place == n, ref.at[:, pl.ds(start, chunk)]) for n, ref in enumerate(refs)]


class Rows:
    def __init__(self, array, part):
        self.array, self.part = array, part


def start_one(choices, target, sem):
    for flag, ref in choices:
        copy = pltpu.make_async_copy(ref, target, sem)
        if flag is None:
            copy.start()
        else:
            pl.when(flag)(copy.start)
    return copy


def stage_kernel(plan, table, *refs):
    tiles, pieces, rows, chunk, has_total, tails = plan
    refs = list(refs)
    sources = [[refs.pop(0) for _ in tile.arrays] for tile in tiles]
    blocks = [[refs.pop(0) for _ in piece] for piece, _ in pieces]
    total_in = refs.pop(0) if has_total else None
    if tails:
        tail_refs = [[refs.pop(0) for _ in range(n)] for n in tails]
        proj_in = refs.pop(0)
    out, grads, weights, total, sems = [refs.pop(0) for _ in range(5)]
    if tails:
        tail_vmem, proj_vmem, tail_sems = refs
    units = weights.shape[1]
    inner = table[0] == 1

    def start_total(t):
        where = pl.ds(t * rows, rows)
        return start_one([(None, total_in.at[where, :])], total.at[where, :], sems.at[len(pieces), t])

    def start_grads(k, t):
        return start_one(tiles[t].copies(sources[t], table, k, chunk), grads.at[k, t], sems.at[k, t])

    def start_piece(k):
        block = blocks[k]
        if pieces[k][1] is not None:
            block = [block[0].at[pl.ds(pieces[k][1] * units, units), :]]
        choices = [(None, block[0])]
        if len(block) > 1:
            choices = [(inner, block[0]), (jnp.logical_not(inner), block[1])]
        return start_one(choices, weights.at[k], sems.at[k, len(tiles)])

    if not tails:
        copies = [[start_piece(k)] + [start_grads(k, t) for t in range(len(tiles))] for k in range(len(pieces))]
        for k in range(len(pieces)):
            for copy in copies[k]:
                copy.wait()
            for t in range(len(tiles)):
                term = dot_t(grads[k, t], weights[k])
                where = pl.ds(t * rows, rows)
                if k > 0:
                    out[where, :] += term
                else:
                    out[where, :] = term
        return

    shared = [start_piece(k) for k in range(len(pieces))]
    shared.append(
        start_one(
            [(None, proj_in.at[:, pl.ds(pl.multiple_of(table[1], 128), units)])], proj_vmem, tail_sems.at[len(tails), 0]
        )
    )
    copies = []
    for t, pair in enumerate(tail_refs):
        mine = [start_grads(k, t) for k in range(len(pieces))] + [start_total(t)]
        for which in range(2):
            ref = pair[which] if len(pair) == 2 else pair[0].at[which]
            mine.append(start_one([(None, ref)], tail_vmem.at[t, which], tail_sems.at[t, which]))
        copies.append(mine)
    for copy in shared:
        copy.wait()
    for t in range(len(tiles)):
        for copy in copies[t]:
            copy.wait()
        where = pl.ds(t * rows, rows)
        value = total[where, :]
        for k in range(len(pieces)):
            value = value + dot_t(grads[k, t], weights[k])
        wide = tail_vmem[t, 1].astype(f32)
        logistic = 0.5 + 0.5 * jnp.tanh(0.5 * wide)
        scaled = value * tail_vmem[t, 0].astype(f32) * logistic * (1.0 + wide * (1.0 - logistic))
        out[where, :] = dot_t(scaled.astype(bf16), proj_vmem[...])


def stage(table, tiles, pieces, rows, total=None, tails=None, proj=None):
    parts = [p.part if isinstance(p, Rows) else None for p in pieces]
    pieces = [p.array if isinstance(p, Rows) else p for p in pieces]
    pieces = [p if isinstance(p, tuple) else (p,) for p in pieces]
    units, chunk = pieces[0][0].shape
    units = units if parts[0] is None else units // 2
    operands = [v for tile in tiles for v in tile.arrays] + [v for p in pieces for v in p]
    width = units
    if total is not None:
        operands.append(total)
    scratch = [
        pltpu.VMEM((len(pieces), len(tiles), rows, chunk), bf16),
        pltpu.VMEM((len(pieces), units, chunk), bf16),
        pltpu.VMEM((len(tiles) * rows, units) if total is not None else (8, 128), f32),
        pltpu.SemaphoreType.DMA((len(pieces) + 1, len(tiles) + 1)),
    ]
    if tails is not None:
        tails = [tail if isinstance(tail, tuple) else (tail,) for tail in tails]
        operands += [v for tail in tails for v in tail] + [proj]
        width = proj.shape[0]
        scratch += [
            pltpu.VMEM((len(tiles), 2, rows, units), bf16),
            pltpu.VMEM((width, units), bf16),
            pltpu.SemaphoreType.DMA((len(tails) + 1, 2)),
        ]
    plan = (tiles, list(zip(pieces, parts)), rows, chunk, total is not None, [len(tail) for tail in tails] if tails else None)
    height = len(tiles) * rows
    return pl.pallas_call(
        functools.partial(stage_kernel, plan),
        out_shape=jax.ShapeDtypeStruct((height, width), f32),
        in_specs=[pl.BlockSpec(memory_space=pltpu.SMEM)] + [pl.BlockSpec(memory_space=pltpu.HBM)] * len(operands),
        out_specs=pl.BlockSpec(memory_space=pltpu.VMEM),
        scratch_shapes=scratch,
        compiler_params=pltpu.CompilerParams(vmem_limit_bytes=50 * 2**20),
        cost_estimate=pl.CostEstimate(
            flops=0,
            bytes_accessed=0,
            transcendentals=0,
        ),
    )(table, *operands)


def highest(left, right, dims):
    return lax.dot_general(
        left, right, (dims, ((), ())), precision=lax.Precision.HIGHEST, preferred_element_type=f32
    )


def inverse_factor(core, out):
    size, step = core.shape[0], 8
    shape = (step, size)
    lane = lax.broadcasted_iota(jnp.int32, shape, 1)
    row = lax.broadcasted_iota(jnp.int32, shape, 0)
    count = size // step
    left = [core[step * n : step * n + step, :] for n in range(count)]
    right = [jnp.where(lane == row + step * n, 1.0, 0.0) for n in range(count)]
    for b in range(count):
        columns = [
            {n: jnp.broadcast_to(left[n][:, step * b + j : step * b + j + 1], shape) for n in range(b, count)}
            for j in range(step)
        ]
        leads = [jnp.broadcast_to(left[b][j : j + 1, :], shape) for j in range(step)]
        twins = [jnp.broadcast_to(right[b][j : j + 1, :], shape) for j in range(step)]
        entry = [[jnp.broadcast_to(columns[j][b][i : i + 1, :], shape) for j in range(i + 1)] for i in range(step)]
        roots = []
        for k in range(step):
            pivot = entry[k][k]
            root = lax.rsqrt(pivot)
            root = root * (1.5 - 0.5 * pivot * root * root)
            roots.append(root)
            for i in range(k + 1, step):
                entry[i][k] = entry[i][k] * root
            for i in range(k + 1, step):
                for j in range(k + 1, i + 1):
                    entry[i][j] = entry[i][j] - entry[i][k] * entry[j][k]
        for k in range(step):
            leads[k], twins[k] = leads[k] * roots[k], twins[k] * roots[k]
            for j in range(k + 1, step):
                leads[j] = leads[j] - entry[j][k] * leads[k]
                twins[j] = twins[j] - entry[j][k] * twins[k]
        done = twins[0]
        for k in range(1, step):
            done = jnp.where(row == k, twins[k], done)
        out[step * b : step * b + step, :] = done
        for n in range(b + 1, count):
            for k in range(step):
                share = columns[k][n] * roots[k]
                for j in range(k + 1, step):
                    columns[j][n] = columns[j][n] - share * entry[j][k]
                left[n] = left[n] - share * leads[k]
                right[n] = right[n] - share * twins[k]


def factor_kernel(place, proj, omega, gram_in, out, inverse):
    rows = out.shape[0]
    overlap = dot_t(proj[...], proj[...])
    wide = jnp.dot(proj[...], omega[...], preferred_element_type=f32)
    coeff = wide.astype(bf16)
    known = coeff.astype(f32)
    square_sum = jnp.sum(overlap * highest(known, known, ((1,), (1,))), keepdims=True)
    gram = gram_in[...]
    diagonal = lax.broadcasted_iota(jnp.int32, gram.shape, 0) == lax.broadcasted_iota(jnp.int32, gram.shape, 1)
    omega_sq = jnp.sum(jnp.where(diagonal, gram, 0.0), keepdims=True)
    shift = shift_scale * jnp.sqrt(square_sum / (omega_sq + tiny_value))
    core = highest(wide, known, ((0,), (0,))) + shift * gram
    core = 0.5 * (core + core.T)
    inverse_factor(core, inverse)
    start = pl.multiple_of(place[0] * rows, rows)
    sketch = lax.dot_general(
        proj[:, pl.ds(start, rows)], coeff, (((0,), (0,)), ((), ())), preferred_element_type=f32
    )
    shifted = sketch + shift * omega[pl.ds(start, rows), :].astype(f32)
    out[...] = highest(shifted, inverse[...], ((1,), (1,)))


def factor_rows(proj_grad, test_matrix, gram, place, rows):
    rank_cols = test_matrix.shape[1]
    return pl.pallas_call(
        factor_kernel,
        out_shape=jax.ShapeDtypeStruct((rows, rank_cols), f32),
        in_specs=[pl.BlockSpec(memory_space=pltpu.SMEM)] + [pl.BlockSpec(memory_space=pltpu.VMEM)] * 3,
        out_specs=pl.BlockSpec(memory_space=pltpu.VMEM),
        scratch_shapes=[
            pltpu.VMEM((rank_cols, rank_cols), f32),
        ],
        compiler_params=pltpu.CompilerParams(vmem_limit_bytes=32 * 2**20),
    )(place.astype(jnp.int32).reshape(1), proj_grad, test_matrix, gram)


def local(tokens, grad_out, gate_pre, up_value, down_weight, in_proj, out_proj, test_matrix):
    z, y, x, c = (lax.axis_index(a) for a in ("z", "y", "x", "c"))
    middle = lax.axis_size("m")
    rows, width = grad_out.shape
    pdim = in_proj.shape[0]
    chunk = down_weight.shape[1] * middle
    if middle > 1:
        down_weight = lax.all_gather(down_weight, "m", axis=1, tiled=True)
        grad_out = grad_out.reshape(rows, LINE, middle, 2, -1).swapaxes(2, 3).reshape(rows, -1)
    half = down_weight.shape[0] // 2
    moved = half * 5 // 14 // 128 * 128
    stay = half - moved
    inner = (z > 0) & (z < LINE - 1)
    PAIR = [(0, 1), (1, 0), (2, 3), (3, 2)]
    IN, OUT, ACROSS = [(0, 1), (3, 2)], [(1, 0), (2, 3)], [(1, 2), (2, 1)]

    def along(value, pairs):
        return lax.ppermute(value, "z", pairs)

    def cut(value, index, dim, kept):
        start = index * half + (moved if kept else 0)
        return lax.dynamic_slice_in_dim(value, start, stay if kept else moved, dim)

    def both_values(index, kept):
        return jnp.stack((cut(up_value, index, 1, kept), cut(gate_pre, index, 1, kept)))

    quarter = width // 4
    k_own = cut(down_weight, y, 0, True)
    k_near, k_mid = along(k_own, PAIR), along(k_own, ACROSS)
    kt_own = swap(cut(down_weight, 1 - y, 0, True), "y")
    o_own, ot_send = cut(down_weight, y, 0, False), cut(down_weight, 1 - y, 0, False)
    sent = lax.dynamic_slice_in_dim(grad_out, (x * 2 + c) * quarter, quarter, 1)
    values_o, values_os = both_values(y, False), both_values(1 - y, False)
    k_own, k_near, k_mid, kt_own, o_own, ot_send, sent, values_o, values_os = settle(
        k_own, k_near, k_mid, kt_own, o_own, ot_send, sent, values_o, values_os
    )

    kt_near, kt_mid = along(kt_own, PAIR), along(kt_own, ACROSS)
    sent_y = swap(sent, "y")
    values_k, values_ks = both_values(y, True), both_values(1 - y, True)
    gram = lax.dot_general(
        test_matrix, test_matrix, (((0,), (0,)), ((), ())), preferred_element_type=f32
    )
    kt_near, kt_mid, sent_y, values_k, values_ks, sent, k_mid, k_near, ot_send, gram = settle(
        kt_near, kt_mid, sent_y, values_k, values_ks, sent, k_mid, k_near, ot_send, gram
    )

    grads_e, k_second, k_far = along(sent, IN), along(k_mid, OUT), along(k_near, ACROSS)
    ot_own = swap(ot_send, "y")
    sent_yx = swap(sent_y, "x")
    act_part = dot_t(tokens, in_proj)
    values_ks0 = swap(values_ks[0], "y")
    grads_e, k_second, k_far, ot_own, sent_y, sent_yx, act_part, kt_mid, kt_near, o_own = settle(
        grads_e, k_second, k_far, ot_own, sent_y, sent_yx, act_part, kt_mid, kt_near, o_own
    )

    o_both = jnp.concatenate((o_own, ot_own), 0)
    o_end, kt_second, kt_far = along(o_both, IN), along(kt_mid, OUT), along(kt_near, ACROSS)
    grads_ey = swap(grads_e, "y")
    grads_ex = swap(grads_e, "x")
    grads_y = (sent_y, swap(sent_y, "c"), sent_yx, swap(sent_yx, "c"))
    (o_end, kt_second, kt_far, grads_e, grads_ex, grads_ey, o_both, k_far, values_o, values_os, values_ks0, values_ks) = settle(
        o_end, kt_second, kt_far, grads_e, grads_ex, grads_ey, o_both, k_far, values_o, values_os, values_ks0, values_ks
    )

    values_e, k_third, o_mid = along(values_o, IN), along(k_far, OUT), along(o_both, ACROSS)
    values_oy = swap(values_os, "y")
    grads_eyx = swap(grads_ey, "x")
    own = x * 2 + c
    near = jnp.where(z % 2 == 0, z + 1, z - 1)
    other = jnp.where(z < 2, 2, 1)
    far = jnp.where(z < 2, 3, 0)

    def table(start, *chunks):
        values = [inner.astype(jnp.int32), start]
        for at, side in chunks:
            at = at * 2 + side
            values += [at, (at // 2) ^ own, at % 2]
        return jnp.stack([jnp.asarray(v, jnp.int32) for v in values])

    def slots(count, skip):
        return [2 + 3 * k + skip for k in range(count)]

    yt = 1 - y
    first = ((z, y), (z, yt), (near, y), (near, yt), (other, y), (other, yt))
    last = ((far, y), (far, yt))
    table_first = table(0, *first)

    def near_tiles(n):
        return [Columns(grad_out, slots(n, 0)), Quarters(grads_y, slots(n, 1))]

    def far_tiles(n):
        return [Quarters(arrays, slots(n, 1)) for arrays in grads_far]

    k_pieces = [k_own, kt_own, k_near, kt_near, (k_mid, k_second), (kt_mid, kt_second)]
    k_total = stage(table_first, near_tiles(6), k_pieces, rows)
    k_total, grads_e, grads_ex = settle(k_total, grads_e, grads_ex)
    grads_far = [(grads_e, swap(grads_e, "c"), grads_ex, swap(grads_ex, "c"))]
    (values_e, k_third, o_mid, values_oy, grads_ey, grads_eyx, k_total, o_end, kt_far, values_ks) = settle(
        values_e, k_third, o_mid, values_oy, grads_ey, grads_eyx, k_total, o_end, kt_far, values_ks
    )

    values_ey, kt_third, o_far = along(values_oy, IN), along(kt_far, OUT), along(o_end, ACROSS)
    values_ks1 = swap(values_ks[1], "y")
    values_ky = (values_ks0, values_ks1)
    grads_far.append((grads_ey, swap(grads_ey, "c"), grads_eyx, swap(grads_eyx, "c")))
    o_total = stage(table_first, near_tiles(6) + far_tiles(6), [o_own, ot_own, Rows(o_end, 0), Rows(o_end, 1), Rows(o_mid, 0), Rows(o_mid, 1)], rows)
    o_total, values_ey, kt_third, o_far = settle(o_total, values_ey, kt_third, o_far)
    out_k = stage(
        table(y * half + moved, *last), near_tiles(2), [(k_far, k_third), (kt_far, kt_third)], rows, k_total,
        [values_k, values_ky], out_proj,
    )
    out_o = stage(
        table(y * half, *last), near_tiles(2) + far_tiles(2), [Rows(o_far, 0), Rows(o_far, 1)], rows, o_total,
        [values_o, values_oy, values_e, values_ey], out_proj,
    )

    act_blocks = act_part.reshape(2, 2, SEQ_LEN, pdim)
    act_kept = lax.dynamic_index_in_dim(act_blocks, c, 1, False) + swap(
        lax.dynamic_index_in_dim(act_blocks, 1 - c, 1, False), "c"
    )
    act_seq = (
        lax.dynamic_index_in_dim(act_kept, x, 0, False)
        + swap(lax.dynamic_index_in_dim(act_kept, 1 - x, 0, False), "x")
    ).astype(bf16)

    out_o = out_o.reshape(2, 2 * rows, pdim)
    blocks = jnp.stack((out_k + jnp.where(inner, out_o[0], 0.0), out_o[1])).reshape(2, 2, 2, 2, SEQ_LEN, pdim)
    kept = lax.dynamic_index_in_dim(blocks, c, 3, False) + swap(
        lax.dynamic_index_in_dim(blocks, 1 - c, 3, False), "c"
    )
    own_x = lax.dynamic_index_in_dim(kept, x, 2, False)
    other_x = lax.dynamic_index_in_dim(kept, 1 - x, 2, False)
    out_sum = own_x[:, 0] + swap(other_x[:, 0], "x") + swap(own_x[:, 1], "y") + swap(other_x[:, 1], ("y", "x"))
    out_seq = (out_sum[0] + lax.ppermute(out_sum[1], "z", [(1, 0), (2, 3)])).astype(bf16)

    proj_own = lax.dot_general(
        act_seq, out_seq, (((0,), (0,)), ((), ())), preferred_element_type=f32
    ).astype(bf16)
    gathered = [proj_own] + [
        lax.ppermute(proj_own, "z", [(i, (i + d) % LINE) for i in range(LINE)]) for d in range(1, LINE)
    ]
    gathered = jnp.stack(gathered)
    if middle > 1:
        gathered = lax.all_gather(gathered, "m", axis=0, tiled=True)
    gathered = jnp.concatenate((gathered, swap(gathered, "x"), swap(gathered, "y"), swap(gathered, ("y", "x"))), 0)
    gathered = jnp.concatenate((gathered, swap(gathered, "c")), 0)
    seqs = gathered.shape[0]
    proj_grad = gathered.reshape(seqs, pdim * pdim)

    own_index = lax.axis_index(("z", "m", "y", "x", "c"))
    own_width = pdim * pdim // (LINE * middle * 8)
    return factor_rows(proj_grad, test_matrix, gram, own_index, own_width)


def solution(mesh):
    dp, tensor = mesh.shape["dp"], mesh.shape["tensor"]
    grid = Mesh(
        mesh.devices.reshape(LINE, dp // (2 * LINE), 2, tensor // 2, 2), ("z", "m", "y", "x", "c")
    )
    dps, tensors = ("z", "m", "y"), ("x", "c")
    in_specs = (
        P(dps, tensors),
        P(dps, None),
        P(dps, tensors),
        P(dps, tensors),
        P(tensors, dps),
        P(None, tensors),
        P(None, tensors),
        P(),
    )
    out_specs = P(dps + tensors, None)
    return jax.shard_map(local, mesh=grid, in_specs=in_specs, out_specs=out_specs, check_vma=False)
```
